512 devices in a mesh: row: 64 (over x, z, y_hi), col: 8 (over y_lo, core).
Axes of the slice: x: 4, y: 8 (y_hi: 2, y_lo: 4; y = y_hi * 4 + y_lo), z: 8, core: 2. Of those that a mesh axis runs over, the one named last changes fastest.
Arguments:
- matrix: float32 [65536, 2048], P('row', 'col'), may hold values from -6 to 6
- signs: int32 [65536], P('row'), may hold values from -1 to 1, as said below
- picks: int32 [16384], P('row'), may hold values from 0 to 65535, as said below
Outputs:
- sketch: float32 [16384, 2048], P('row', 'col')
- gram: float32 [2048, 2048], P('row', 'col')
The draws below stay inside these ranges and needn't reach their ends.
Inputs may be any that keep to these rules, and one draw needn't show every extreme that they name: `signs`: each entry is +1 or -1. `picks`: sorted and distinct; entries k * 256 to (k + 1) * 256 - 1 lie in rows k * 1024 to (k + 1) * 1024 - 1.
All inputs are finite; a program needn't handle non-finite values.
Results may differ from the reference program's by a relative error of at most 0.00013.
Values sent between devices are 32-bit elements; how exact they have to be, the bound alone decides.
No kernel may reach another device: no remote copies, remote signals or barrier semaphores. Data moves between devices by JAX's collectives and lax.ppermute only.
A program may use at most 64 MiB of HBM per device.

```python
import jax
import jax.numpy as jnp
from jax import lax

NCOL = 2048
ROWS_DEV = 1024
S_DEV = 256
ROWS = 65536
SAMPLES = 16384


def draw_signs(key, part):
    key = jax.random.fold_in(key, 11)
    bits = jax.random.randint(key, (ROWS,), 0, 2)
    return (2 * bits - 1).astype(jnp.int32)


def draw_picks(key, part):
    key = jax.random.fold_in(key, 23)
    blocks = SAMPLES // S_DEV
    block_keys = jax.random.split(key, blocks)

    def pick_block(block_key):
        order = jax.random.permutation(block_key, ROWS_DEV)
        return jnp.sort(order[:S_DEV])
    chosen = jax.vmap(pick_block)(block_keys)
    starts = (jnp.arange(blocks, dtype=jnp.int32) * ROWS_DEV)[:, None]
    return (chosen.astype(jnp.int32) + starts).reshape(SAMPLES).astype(jnp.int32)


def block_levels(own_key, shape, pieces, smallest, high):
    def one(axis_at, blocks):
        heights = jax.random.uniform(jax.random.fold_in(jax.random.fold_in(own_key, 6), axis_at), (blocks,), jnp.float32, smallest / len(pieces), high / len(pieces))
        return jnp.repeat(jnp.exp(heights), shape[axis_at] // blocks).reshape((-1,) + (1,) * (len(shape) - axis_at - 1))

    loudness = one(*pieces[0])
    for cut in pieces[1:]:
        loudness = loudness * one(*cut)
    return loudness


def gaussian(stream_key, shape, scale, reach, cuts=(), held_as=jnp.bfloat16):
    array = scale * jax.random.normal(stream_key, shape, jnp.float32)
    if cuts:
        array = array * block_levels(stream_key, shape, cuts, -0.22, 0.18)
    return jnp.clip(array, -reach, reach).astype(held_as)


def setup_inputs(seed: int = 0) -> dict:
    key_of = jax.random.split(jax.random.key(seed), 4)
    matrix = gaussian(key_of[0], (ROWS, NCOL), 1.0, 6.0, ((0, 64), (1, 8)), jnp.float32)
    signs = draw_signs(jax.random.fold_in(key_of[3], 71), 0)
    picks = draw_picks(jax.random.fold_in(key_of[3], 71), 0)
    return {"matrix": matrix, "signs": signs, "picks": picks}


def transform(values):
    total = values.shape[0]
    width = values.shape[1]
    half = 1
    while half < total:
        grouped = values.reshape(total // (2 * half), 2, half, width)
        first = grouped[:, 0]
        second = grouped[:, 1]
        values = jnp.stack([first + second, first - second], axis=1).reshape(total, width)
        half = half * 2
    return values


def reference(matrix, signs, picks):
    signed = matrix * signs.astype(jnp.float32)[:, None]
    mixed = transform(signed) * jnp.float32(1.0 / (ROWS ** 0.5))
    sketch = jnp.take(mixed, picks.astype(jnp.int32), axis=0)
    gram = jnp.dot(sketch.T, sketch, precision=lax.Precision.HIGHEST, preferred_element_type=jnp.float32) / jnp.float32(SAMPLES)
    return sketch, gram
```

```python
import functools

import jax
import jax.numpy as jnp
import numpy as np
from jax import lax
from jax.experimental import pallas as pl
from jax.experimental.pallas import tpu as pltpu
from jax.sharding import PartitionSpec as P

F32 = jnp.float32
BF16 = jnp.bfloat16
GROUPS = 64
LANES = 512
VMEM_LIMIT = 48 * 1024 * 1024


def sylvester(order):
    both = np.arange(order)[:, None] & np.arange(order)[None, :]
    parity = np.zeros_like(both)
    while both.any():
        parity ^= both & 1
        both >>= 1
    return (1 - 2 * parity).astype(np.float32)


def split(x):
    high = x.astype(BF16)
    return high, (x - high.astype(F32)).astype(BF16)


def dot(a, b):
    return jnp.dot(a, b, preferred_element_type=F32)


def chunk_kernel(matrix_ref, signs_ref, out_ref):
    signed = (matrix_ref[...] * signs_ref[...].astype(F32)).T
    for half in range(2):
        for v in range(4):
            start = half * LANES + v * 128
            for q in range(4):
                out_ref[pl.ds(v * 8 + half * 4 + q, GROUPS, stride=32), :] = signed[
                    q * GROUPS : (q + 1) * GROUPS, start : start + 128
                ]


def mix_kernel(chunks_ref, block_table_ref, lane_table_ref, picks_ref, out_ref, mixed):
    received = jnp.concatenate(
        [chunks_ref[:, v * 8 : v * 8 + 8, :].reshape(8 * GROUPS, 128) for v in range(4)], axis=1
    )
    high, low = split(received)
    table = block_table_ref[...]
    high, low = split(dot(table, high) + dot(table, low))
    table = lane_table_ref[...]
    mixed[...] = (dot(high, table) + dot(low, table)) * F32(2.0**-8)
    first = lax.broadcasted_iota(jnp.int32, (8, 128), 0) < 4

    def eight(group, carry):
        base = pl.multiple_of(group * 8, 8)
        owner = base + lax.broadcasted_iota(jnp.int32, (8, 256), 0)
        local_picks = picks_ref[pl.ds(base, 8), :] - owner * 1024
        for inner in range(8):
            rows = pl.ds(pl.multiple_of((base + inner) * 8, 8), 8)
            sources = [mixed[rows, v * 128 : v * 128 + 128] for v in range(4)]
            found = []
            for part in range(2):
                local = jnp.broadcast_to(
                    local_picks[inner : inner + 1, part * 128 : part * 128 + 128], (8, 128)
                )
                lane = jnp.bitwise_and(local, 127)
                vreg = jnp.bitwise_and(jnp.right_shift(local, 7), 3)
                got = None
                for v in range(4):
                    here = jnp.take_along_axis(sources[v], lane, axis=1)
                    got = here if got is None else jnp.where(vreg == v, here, got)
                found.append((got, jnp.right_shift(local, 9) == 1))
            (a, up_a), (b, up_b) = found
            out_ref[rows, :] = jnp.where(
                first,
                jnp.where(up_a, pltpu.roll(a, 4, 0), a),
                jnp.where(up_b, b, pltpu.roll(b, 4, 0)),
            )
        return carry

    lax.fori_loop(0, GROUPS // 8, eight, 0)


def order_kernel(got_ref, across_ref, sketch_ref):
    for q in range(4):
        for part in range(2):
            across_ref[q * GROUPS : (q + 1) * GROUPS, part * 128 : part * 128 + 128] = got_ref[
                pl.ds(part * 4 + q, GROUPS, stride=8), :
            ]
    sketch_ref[...] = across_ref[...].T


def gram_kernel(order, me_ref, sketch_ref, *refs):
    parts, out_ref = refs[:-1], refs[-1]
    me = me_ref[0]
    right_high, right_low = split(sketch_ref[...])
    width = sketch_ref.shape[1]
    block = 0
    for part in parts:
        for piece in range(part.shape[0] // width):
            left_high, left_low = split(part[piece * width : (piece + 1) * width, :])
            product = dot(left_high, right_high) + dot(left_high, right_low) + dot(left_low, right_high)
            place = pl.multiple_of(jnp.bitwise_xor(me, order[block]) * width, width)
            out_ref[pl.ds(place, width), :] = product
            block += 1


def call(kernel, out_shape, scratch=(), **more):
    vmem = pl.BlockSpec(memory_space=pltpu.VMEM)
    many = isinstance(out_shape, (list, tuple))
    return pl.pallas_call(
        kernel,
        out_shape=out_shape,
        out_specs=[vmem] * len(out_shape) if many else vmem,
        scratch_shapes=list(scratch),
        compiler_params=pltpu.CompilerParams(vmem_limit_bytes=VMEM_LIMIT),
        **more,
    )


def shape(*dims):
    return jax.ShapeDtypeStruct(dims, F32)


def from_partner(x, axis, distance):
    return lax.ppermute(x, axis, [(i, i ^ distance) for i in range(lax.axis_size(axis))])


def shards(matrix, signs, picks):
    all_picks = lax.all_gather(picks, "row", axis=0, tiled=False)
    chunks = call(chunk_kernel, shape(32 * GROUPS, 128))(matrix, signs[:, None])
    chunks = lax.all_to_all(chunks.reshape(GROUPS, 32, 128), "row", 0, 0, tiled=True)
    block_table = jnp.asarray(np.kron(sylvester(2 * GROUPS), np.eye(4)), BF16)
    lane_table = jnp.asarray(sylvester(LANES), BF16)
    picked = call(mix_kernel, shape(8 * GROUPS, 128), [pltpu.VMEM((8 * GROUPS, LANES), F32)])(
        chunks, block_table, lane_table, all_picks
    )
    picked = lax.all_to_all(picked, "row", 0, 0, tiled=True)
    across, sketch = call(order_kernel, [shape(256, 256), shape(256, 256)])(picked)

    pieces = [across]
    for distance in (4, 2, 1):
        held = pieces[0] if len(pieces) == 1 else jnp.concatenate(pieces, 0)
        pieces.append(from_partner(held, "col", distance))
    me = lax.axis_index("col").astype(jnp.int32)[None]
    vmem = pl.BlockSpec(memory_space=pltpu.VMEM)
    kernel = functools.partial(gram_kernel, (0, 4, 2, 6, 1, 5, 3, 7))
    gram = call(
        kernel,
        shape(2048, 256),
        in_specs=[pl.BlockSpec(memory_space=pltpu.SMEM)] + [vmem] * 5,
    )(me, sketch, *pieces)

    x_groups = [[x * 16 + i for x in range(4)] for i in range(16)]
    rest_groups = [[x * 16 + i for i in range(16)] for x in range(4)]
    gram = lax.all_to_all(gram, "row", 0, 0, axis_index_groups=x_groups, tiled=True)
    gram = jnp.sum(gram.reshape(4, 512, 256), 0)
    gram = lax.all_to_all(gram, "row", 0, 0, axis_index_groups=rest_groups, tiled=True)
    gram = jnp.sum(gram.reshape(16, 32, 256), 0) * F32(2.0**-14)
    return sketch, gram


def solution(mesh):
    placed = (P("row", "col"), P("row"), P("row"))
    return jax.shard_map(
        shards,
        mesh=mesh,
        in_specs=placed,
        out_specs=(P("row", "col"), P("row", "col")),
        check_vma=False,
    )
```

```python
import functools

import jax
import jax.numpy as jnp
import numpy as np
from jax import lax
from jax.experimental import pallas as pl
from jax.experimental.pallas import tpu as pltpu
from jax.sharding import PartitionSpec as P

F32 = jnp.float32
BF16 = jnp.bfloat16
GROUPS = 64
LANES = 512
CHUNK = 40
VMEM_LIMIT = 48 * 1024 * 1024


def sylvester(order):
    both = np.arange(order)[:, None] & np.arange(order)[None, :]
    parity = np.zeros_like(both)
    while both.any():
        parity ^= both & 1
        both >>= 1
    return (1 - 2 * parity).astype(np.float32)


def split(x):
    high = x.astype(BF16)
    return high, (x - high.astype(F32)).astype(BF16)


def dot(a, b):
    return jnp.dot(a, b, preferred_element_type=F32)


def chunk_kernel(matrix_ref, signs_ref, picks_ref, out_ref):
    signed = (matrix_ref[...] * signs_ref[...].astype(F32)).T
    for half in range(2):
        for v in range(4):
            start = half * LANES + v * 128
            for q in range(4):
                out_ref[pl.ds(v * 8 + half * 4 + q, GROUPS, stride=CHUNK), :] = signed[
                    q * GROUPS : (q + 1) * GROUPS, start : start + 128
                ]
    for part in range(8):
        if part < 2:
            row = picks_ref[:, part * 128 : part * 128 + 128].astype(F32)
        else:
            row = jnp.zeros((1, 128), F32)
        out_ref[pl.ds(32 + part, GROUPS, stride=CHUNK), :] = jnp.broadcast_to(row, (GROUPS, 128))


def mix_kernel(chunks_ref, block_table_ref, lane_table_ref, out_ref, mixed):
    received = jnp.concatenate(
        [chunks_ref[:, v * 8 : v * 8 + 8, :].reshape(8 * GROUPS, 128) for v in range(4)], axis=1
    )
    high, low = split(received)
    table = block_table_ref[...]
    high, low = split(dot(table, high) + dot(table, low))
    table = lane_table_ref[...]
    mixed[...] = (dot(high, table) + dot(low, table)) * F32(2.0**-8)
    first = lax.broadcasted_iota(jnp.int32, (8, 128), 0) < 4

    def eight(group, carry):
        for inner in range(8):
            block = group * 8 + inner
            rows = pl.ds(pl.multiple_of(block * 8, 8), 8)
            local_picks = chunks_ref[block, 32:40, :].astype(jnp.int32)
            sources = [mixed[rows, v * 128 : v * 128 + 128] for v in range(4)]
            found = []
            for part in range(2):
                local = jnp.broadcast_to(
                    local_picks[part : part + 1, :], (8, 128)
                )
                lane = jnp.bitwise_and(local, 127)
                vreg = jnp.bitwise_and(jnp.right_shift(local, 7), 3)
                got = None
                for v in range(4):
                    here = jnp.take_along_axis(sources[v], lane, axis=1)
                    got = here if got is None else jnp.where(vreg == v, here, got)
                found.append((got, jnp.right_shift(local, 9) == 1))
            (a, up_a), (b, up_b) = found
            out_ref[rows, :] = jnp.where(
                first,
                jnp.where(up_a, pltpu.roll(a, 4, 0), a),
                jnp.where(up_b, b, pltpu.roll(b, 4, 0)),
            )
        return carry

    lax.fori_loop(0, GROUPS // 8, eight, 0)


def order_kernel(got_ref, across_ref, sketch_ref):
    for q in range(4):
        for part in range(2):
            across_ref[q * GROUPS : (q + 1) * GROUPS, part * 128 : part * 128 + 128] = got_ref[
                pl.ds(part * 4 + q, GROUPS, stride=8), :
            ]
    sketch_ref[...] = across_ref[...].T


def gram_kernel(order, me_ref, sketch_ref, *refs):
    parts, out_ref = refs[:-1], refs[-1]
    me = me_ref[0]
    right_high, right_low = split(sketch_ref[...])
    width = sketch_ref.shape[1]
    block = 0
    for part in parts:
        for piece in range(part.shape[0] // width):
            left_high, left_low = split(part[piece * width : (piece + 1) * width, :])
            product = dot(left_high, right_high) + dot(left_high, right_low) + dot(left_low, right_high)
            place = pl.multiple_of(jnp.bitwise_xor(me, order[block]) * width, width)
            out_ref[pl.ds(place, width), :] = product
            block += 1


def call(kernel, out_shape, scratch=(), **more):
    vmem = pl.BlockSpec(memory_space=pltpu.VMEM)
    many = isinstance(out_shape, (list, tuple))
    return pl.pallas_call(
        kernel,
        out_shape=out_shape,
        out_specs=[vmem] * len(out_shape) if many else vmem,
        scratch_shapes=list(scratch),
        compiler_params=pltpu.CompilerParams(vmem_limit_bytes=VMEM_LIMIT),
        **more,
    )


def shape(*dims):
    return jax.ShapeDtypeStruct(dims, F32)


def from_partner(x, axis, distance):
    return lax.ppermute(x, axis, [(i, i ^ distance) for i in range(lax.axis_size(axis))])


def shards(matrix, signs, picks):
    offsets = picks - lax.axis_index("row") * matrix.shape[0]
    chunks = call(chunk_kernel, shape(CHUNK * GROUPS, 128))(
        matrix, signs[:, None], offsets[None, :]
    )
    chunks = lax.all_to_all(chunks.reshape(GROUPS, CHUNK, 128), "row", 0, 0, tiled=True)
    block_table = jnp.asarray(np.kron(sylvester(2 * GROUPS), np.eye(4)), BF16)
    lane_table = jnp.asarray(sylvester(LANES), BF16)
    picked = call(mix_kernel, shape(8 * GROUPS, 128), [pltpu.VMEM((8 * GROUPS, LANES), F32)])(
        chunks, block_table, lane_table
    )
    picked = lax.all_to_all(picked, "row", 0, 0, tiled=True)
    across, sketch = call(order_kernel, [shape(256, 256), shape(256, 256)])(picked)

    pieces = [across]
    for distance in (4, 2, 1):
        held = pieces[0] if len(pieces) == 1 else jnp.concatenate(pieces, 0)
        pieces.append(from_partner(held, "col", distance))
    me = lax.axis_index("col").astype(jnp.int32)[None]
    vmem = pl.BlockSpec(memory_space=pltpu.VMEM)
    kernel = functools.partial(gram_kernel, (0, 4, 2, 6, 1, 5, 3, 7))
    gram = call(
        kernel,
        shape(2048, 256),
        in_specs=[pl.BlockSpec(memory_space=pltpu.SMEM)] + [vmem] * 5,
    )(me, sketch, *pieces)

    x_groups = [[x * 16 + i for x in range(4)] for i in range(16)]
    rest_groups = [[x * 16 + i for i in range(16)] for x in range(4)]
    gram = lax.all_to_all(gram, "row", 0, 0, axis_index_groups=x_groups, tiled=True)
    gram = jnp.sum(gram.reshape(4, 512, 256), 0)
    gram = lax.all_to_all(gram, "row", 0, 0, axis_index_groups=rest_groups, tiled=True)
    gram = jnp.sum(gram.reshape(16, 32, 256), 0) * F32(2.0**-14)
    return sketch, gram


def solution(mesh):
    placed = (P("row", "col"), P("row"), P("row"))
    return jax.shard_map(
        shards,
        mesh=mesh,
        in_specs=placed,
        out_specs=(P("row", "col"), P("row", "col")),
        check_vma=False,
    )
```

```python
import functools

import jax
import jax.numpy as jnp
import numpy as np
from jax import lax
from jax.experimental import pallas as pl
from jax.experimental.pallas import tpu as pltpu
from jax.sharding import PartitionSpec as P

F32 = jnp.float32
BF16 = jnp.bfloat16
GROUPS = 64
LANES = 512
TILES = 17
VMEM_LIMIT = 48 * 1024 * 1024


def sylvester(order):
    both = np.arange(order)[:, None] & np.arange(order)[None, :]
    parity = np.zeros_like(both)
    while both.any():
        parity ^= both & 1
        both >>= 1
    return (1 - 2 * parity).astype(np.float32)


def split(x):
    high = x.astype(BF16)
    return high, (x - high.astype(F32)).astype(BF16)


def dot(a, b):
    return jnp.dot(a, b, preferred_element_type=F32)


def chunk_kernel(matrix_ref, signs_ref, picks_ref, out_ref):
    signed = matrix_ref[...].T * signs_ref[...].astype(F32)
    for half in range(2):
        for v in range(4):
            start = half * LANES + v * 128
            for q in range(4):
                out_ref[pl.ds(v * 4 + q, GROUPS, stride=TILES), half, :] = signed[
                    q * GROUPS : (q + 1) * GROUPS, start : start + 128
                ]
    offsets = jnp.bitwise_and(picks_ref[...], 1023).astype(F32)
    for part in range(2):
        out_ref[pl.ds(16, GROUPS, stride=TILES), part, :] = jnp.broadcast_to(
            offsets[part : part + 1, :], (GROUPS, 128)
        )


def mix_kernel(chunks_ref, block_table_ref, lane_table_ref, out_ref, *mixed):
    block_table = block_table_ref[...]
    lane_table = lane_table_ref[...]
    for pair in range(2):
        columns = []
        for v in range(4):
            rows = [
                chunks_ref[pl.ds(v * 4 + q, GROUPS, stride=TILES), half, :]
                for q in (2 * pair, 2 * pair + 1)
                for half in range(2)
            ]
            columns.append(jnp.concatenate(rows, 0))
        high, low = split(jnp.concatenate(columns, 1))
        high, low = split(dot(block_table, high) + dot(block_table, low))
        done = (dot(high, lane_table) + dot(low, lane_table)) * F32(2.0**-8)
        for v in range(4):
            mixed[v][pair * 256 : pair * 256 + 256, :] = done[:, v * 128 : v * 128 + 128]
    even = jnp.bitwise_and(lax.broadcasted_iota(jnp.int32, (8, 128), 0), 1) == 0

    def eight(group, carry):
        for inner in range(8):
            block = group * 8 + inner
            local_picks = chunks_ref[block * TILES + 16].astype(jnp.int32)
            sources = [mixed[v][pl.ds(block, 8, stride=GROUPS), :] for v in range(4)]
            found = []
            for part in range(2):
                local = jnp.broadcast_to(local_picks[part : part + 1, :], (8, 128))
                lane = jnp.bitwise_and(local, 127)
                vreg = jnp.bitwise_and(jnp.right_shift(local, 7), 3)
                got = None
                for v in range(4):
                    here = jnp.take_along_axis(sources[v], lane, axis=1)
                    got = here if got is None else jnp.where(vreg == v, here, got)
                found.append((got, jnp.right_shift(local, 9) == 1))
            (a, up_a), (b, up_b) = found
            out_ref[pl.ds(pl.multiple_of(block * 8, 8), 8), :] = jnp.where(
                even,
                jnp.where(up_a, pltpu.roll(a, 7, 0), a),
                jnp.where(up_b, b, pltpu.roll(b, 1, 0)),
            )
        return carry

    lax.fori_loop(0, GROUPS // 8, eight, 0)


def order_kernel(got_ref, across_ref, sketch_ref):
    for q in range(4):
        for part in range(2):
            across_ref[q * GROUPS : (q + 1) * GROUPS, part * 128 : part * 128 + 128] = got_ref[
                pl.ds(q * 2 + part, GROUPS, stride=8), :
            ]
    sketch_ref[...] = across_ref[...].T


def gram_kernel(order, me_ref, sketch_ref, *refs):
    parts, out_ref = refs[:-1], refs[-1]
    me = me_ref[0]
    right_high, right_low = split(sketch_ref[...])
    width = sketch_ref.shape[1]
    block = 0
    for part in parts:
        for piece in range(part.shape[0] // width):
            left_high, left_low = split(part[piece * width : (piece + 1) * width, :])
            product = dot(left_high, right_high) + dot(left_high, right_low) + dot(left_low, right_high)
            place = pl.multiple_of(jnp.bitwise_xor(me, order[block]) * width, width)
            out_ref[pl.ds(place, width), :] = product
            block += 1


def call(kernel, out_shape, scratch=(), **more):
    vmem = pl.BlockSpec(memory_space=pltpu.VMEM)
    many = isinstance(out_shape, (list, tuple))
    return pl.pallas_call(
        kernel,
        out_shape=out_shape,
        out_specs=[vmem] * len(out_shape) if many else vmem,
        scratch_shapes=list(scratch),
        compiler_params=pltpu.CompilerParams(vmem_limit_bytes=VMEM_LIMIT),
        **more,
    )


def shape(*dims):
    return jax.ShapeDtypeStruct(dims, F32)


def from_partner(x, axis, distance):
    return lax.ppermute(x, axis, [(i, i ^ distance) for i in range(lax.axis_size(axis))])


def shards(matrix, signs, picks):
    chunks = call(chunk_kernel, shape(GROUPS * TILES, 2, 128))(
        matrix, signs[None, :], picks.reshape(2, 128)
    )
    chunks = lax.all_to_all(chunks.reshape(GROUPS, TILES, 2, 128), "row", 0, 0, tiled=True)
    block_table = jnp.asarray(np.kron(np.eye(2), sylvester(2 * GROUPS)), BF16)
    lane_table = jnp.asarray(sylvester(LANES), BF16)
    picked = call(mix_kernel, shape(8 * GROUPS, 128), [pltpu.VMEM((8 * GROUPS, 128), F32)] * 4)(
        chunks.reshape(GROUPS * TILES, 2, 128), block_table, lane_table
    )
    picked = picked.reshape(GROUPS, 8, 128)
    picked = lax.all_to_all(picked, "row", 0, 0, tiled=True).reshape(8 * GROUPS, 128)
    across, sketch = call(order_kernel, [shape(256, 256), shape(256, 256)])(picked)

    pieces = [across]
    for distance in (4, 2, 1):
        held = pieces[0] if len(pieces) == 1 else jnp.concatenate(pieces, 0)
        pieces.append(from_partner(held, "col", distance))
    me = lax.axis_index("col").astype(jnp.int32)[None]
    vmem = pl.BlockSpec(memory_space=pltpu.VMEM)
    kernel = functools.partial(gram_kernel, (0, 4, 2, 6, 1, 5, 3, 7))
    gram = call(
        kernel,
        shape(2048, 256),
        in_specs=[pl.BlockSpec(memory_space=pltpu.SMEM)] + [vmem] * 5,
    )(me, sketch, *pieces)

    x_groups = [[x * 16 + i for x in range(4)] for i in range(16)]
    rest_groups = [[x * 16 + i for i in range(16)] for x in range(4)]
    gram = lax.all_to_all(gram, "row", 0, 0, axis_index_groups=x_groups, tiled=True)
    gram = jnp.sum(gram.reshape(4, 512, 256), 0)
    gram = lax.all_to_all(gram, "row", 0, 0, axis_index_groups=rest_groups, tiled=True)
    gram = jnp.sum(gram.reshape(16, 32, 256), 0) * F32(2.0**-14)
    return sketch, gram


def solution(mesh):
    placed = (P("row", "col"), P("row"), P("row"))
    return jax.shard_map(
        shards,
        mesh=mesh,
        in_specs=placed,
        out_specs=(P("row", "col"), P("row", "col")),
        check_vma=False,
    )
```

```python
import functools

import jax
import jax.numpy as jnp
import numpy as np
from jax import lax
from jax.experimental import pallas as pl
from jax.experimental.pallas import tpu as pltpu
from jax.sharding import PartitionSpec as P

F32 = jnp.float32
BF16 = jnp.bfloat16
GROUPS = 64
LANES = 512
TILES = 17
VMEM_LIMIT = 48 * 1024 * 1024


def sylvester(order):
    both = np.arange(order)[:, None] & np.arange(order)[None, :]
    parity = np.zeros_like(both)
    while both.any():
        parity ^= both & 1
        both >>= 1
    return (1 - 2 * parity).astype(np.float32)


def split(x):
    high = x.astype(BF16)
    return high, (x - high.astype(F32)).astype(BF16)


def dot(a, b):
    return jnp.dot(a, b, preferred_element_type=F32)


def chunk_kernel(matrix_ref, signs_ref, picks_ref, out_ref):
    signed = matrix_ref[...].T * signs_ref[...].astype(F32)
    for half in range(2):
        for v in range(4):
            start = half * LANES + v * 128
            for q in range(4):
                out_ref[pl.ds(v * 4 + q, GROUPS, stride=TILES), half, :] = signed[
                    q * GROUPS : (q + 1) * GROUPS, start : start + 128
                ]
    offsets = jnp.bitwise_and(picks_ref[...], 1023).astype(F32)
    for part in range(2):
        out_ref[pl.ds(16, GROUPS, stride=TILES), part, :] = jnp.broadcast_to(
            offsets[part : part + 1, :], (GROUPS, 128)
        )


def mix_kernel(chunks_ref, block_table_ref, lane_table_ref, out_ref, *mixed):
    block_table = block_table_ref[...]
    lane_table = lane_table_ref[...]
    for pair in range(2):
        columns = []
        for v in range(4):
            rows = [
                chunks_ref[pl.ds(v * 4 + q, GROUPS, stride=TILES), half, :]
                for q in (2 * pair, 2 * pair + 1)
                for half in range(2)
            ]
            columns.append(jnp.concatenate(rows, 0))
        high, low = split(jnp.concatenate(columns, 1))
        high, low = split(dot(block_table, high) + dot(block_table, low))
        done = (dot(high, lane_table) + dot(low, lane_table)) * F32(2.0**-8)
        for v in range(4):
            mixed[v][pair * 256 : pair * 256 + 256, :] = done[:, v * 128 : v * 128 + 128]
    even = jnp.bitwise_and(lax.broadcasted_iota(jnp.int32, (8, 128), 0), 1) == 0

    def eight(group, carry):
        for inner in range(8):
            block = group * 8 + inner
            local_picks = chunks_ref[block * TILES + 16].astype(jnp.int32)
            sources = [mixed[v][pl.ds(block, 8, stride=GROUPS), :] for v in range(4)]
            found = []
            for part in range(2):
                local = jnp.broadcast_to(local_picks[part : part + 1, :], (8, 128))
                lane = jnp.bitwise_and(local, 127)
                vreg = jnp.bitwise_and(jnp.right_shift(local, 7), 3)
                got = None
                for v in range(4):
                    here = jnp.take_along_axis(sources[v], lane, axis=1)
                    got = here if got is None else jnp.where(vreg == v, here, got)
                found.append((got, jnp.right_shift(local, 9) == 1))
            (a, up_a), (b, up_b) = found
            out_ref[pl.ds(pl.multiple_of(block * 8, 8), 8), :] = jnp.where(
                even,
                jnp.where(up_a, pltpu.roll(a, 7, 0), a),
                jnp.where(up_b, b, pltpu.roll(b, 1, 0)),
            )
        return carry

    lax.fori_loop(0, GROUPS // 8, eight, 0)


def order_kernel(got_ref, across_ref, sketch_ref):
    for q in range(4):
        for part in range(2):
            across_ref[q * GROUPS : (q + 1) * GROUPS, part * 128 : part * 128 + 128] = got_ref[
                pl.ds(q * 2 + part, GROUPS, stride=8), :
            ]
    sketch_ref[...] = across_ref[...].T


def gram_kernel(order, me_ref, sketch_ref, *refs):
    parts, out_ref = refs[:-1], refs[-1]
    me = me_ref[0]
    right_high, right_low = split(sketch_ref[...])
    width = sketch_ref.shape[1]
    block = 0
    for part in parts:
        for piece in range(part.shape[0] // width):
            left_high, left_low = split(part[piece * width : (piece + 1) * width, :])
            product = dot(left_high, right_high) + dot(left_high, right_low) + dot(left_low, right_high)
            place = jnp.bitwise_xor(me, order[block])
            place = jnp.right_shift(place, 1) * 512 + jnp.bitwise_and(place, 1) * 128
            for z in range(4):
                start = pl.multiple_of(place + (z % 2) * 256 + (z // 2) * 64, 64)
                out_ref[pl.ds(start, 64), :] = product[z * 64 : z * 64 + 64]
            block += 1


def call(kernel, out_shape, scratch=(), **more):
    vmem = pl.BlockSpec(memory_space=pltpu.VMEM)
    many = isinstance(out_shape, (list, tuple))
    return pl.pallas_call(
        kernel,
        out_shape=out_shape,
        out_specs=[vmem] * len(out_shape) if many else vmem,
        scratch_shapes=list(scratch),
        compiler_params=pltpu.CompilerParams(vmem_limit_bytes=VMEM_LIMIT),
        **more,
    )


def shape(*dims):
    return jax.ShapeDtypeStruct(dims, F32)


def from_partner(x, axis, distance):
    return lax.ppermute(x, axis, [(i, i ^ distance) for i in range(lax.axis_size(axis))])


def shards(matrix, signs, picks):
    chunks = call(chunk_kernel, shape(GROUPS * TILES, 2, 128))(
        matrix, signs[None, :], picks.reshape(2, 128)
    )
    chunks = lax.all_to_all(chunks.reshape(GROUPS, TILES, 2, 128), "row", 0, 0, tiled=True)
    block_table = jnp.asarray(np.kron(np.eye(2), sylvester(2 * GROUPS)), BF16)
    lane_table = jnp.asarray(sylvester(LANES), BF16)
    picked = call(mix_kernel, shape(8 * GROUPS, 128), [pltpu.VMEM((8 * GROUPS, 128), F32)] * 4)(
        chunks.reshape(GROUPS * TILES, 2, 128), block_table, lane_table
    )
    picked = picked.reshape(GROUPS, 8, 128)
    picked = lax.all_to_all(picked, "row", 0, 0, tiled=True).reshape(8 * GROUPS, 128)
    across, sketch = call(order_kernel, [shape(256, 256), shape(256, 256)])(picked)

    pieces = [across]
    for distance in (4, 2, 1):
        held = pieces[0] if len(pieces) == 1 else jnp.concatenate(pieces, 0)
        pieces.append(from_partner(held, "col", distance))
    me = lax.axis_index("col").astype(jnp.int32)[None]
    vmem = pl.BlockSpec(memory_space=pltpu.VMEM)
    kernel = functools.partial(gram_kernel, (0, 4, 2, 6, 1, 5, 3, 7))
    gram = call(
        kernel,
        shape(2048, 256),
        in_specs=[pl.BlockSpec(memory_space=pltpu.SMEM)] + [vmem] * 5,
    )(me, sketch, *pieces)

    near = [[x * 16 + h * 4 + l * 2 + y for x in range(4) for l in range(2)] for h in range(4) for y in range(2)]
    far = [[x * 16 + h * 4 + l * 2 + y for h in range(4) for y in range(2)] for x in range(4) for l in range(2)]
    gram = lax.all_to_all(gram, "row", 0, 0, axis_index_groups=near, tiled=True)
    gram = jnp.sum(gram.reshape(8, 256, 256), 0)
    gram = lax.all_to_all(gram, "row", 0, 0, axis_index_groups=far, tiled=True)
    gram = jnp.sum(gram.reshape(8, 32, 256), 0) * F32(2.0**-14)
    return sketch, gram


def solution(mesh):
    placed = (P("row", "col"), P("row"), P("row"))
    return jax.shard_map(
        shards,
        mesh=mesh,
        in_specs=placed,
        out_specs=(P("row", "col"), P("row", "col")),
        check_vma=False,
    )
```

```python
import functools

import jax
import jax.numpy as jnp
import numpy as np
from jax import lax
from jax.experimental import pallas as pl
from jax.experimental.pallas import tpu as pltpu
from jax.sharding import PartitionSpec as P

F32 = jnp.float32
BF16 = jnp.bfloat16
GROUPS = 64
LANES = 512
TILES = 17
VMEM_LIMIT = 48 * 1024 * 1024


def sylvester(order):
    both = np.arange(order)[:, None] & np.arange(order)[None, :]
    parity = np.zeros_like(both)
    while both.any():
        parity ^= both & 1
        both >>= 1
    return (1 - 2 * parity).astype(np.float32)


def split(x):
    high = x.astype(BF16)
    return high, (x - high.astype(F32)).astype(BF16)


def dot(a, b):
    return jnp.dot(a, b, preferred_element_type=F32)


def chunk_kernel(matrix_ref, signs_ref, picks_ref, out_ref):
    signed = matrix_ref[...].T * signs_ref[...].astype(F32)
    for half in range(2):
        for v in range(4):
            start = half * LANES + v * 128
            for q in range(4):
                out_ref[pl.ds(v * 4 + q, GROUPS, stride=TILES), half, :] = signed[
                    q * GROUPS : (q + 1) * GROUPS, start : start + 128
                ]
    offsets = jnp.bitwise_and(picks_ref[...], 1023).astype(F32)
    for part in range(2):
        out_ref[pl.ds(16, GROUPS, stride=TILES), part, :] = jnp.broadcast_to(
            offsets[part : part + 1, :], (GROUPS, 128)
        )


def mix_kernel(chunks_ref, block_table_ref, lane_table_ref, out_ref, *mixed):
    block_table = block_table_ref[...]
    lane_table = lane_table_ref[...]
    for pair in range(2):
        columns = []
        for v in range(4):
            rows = [
                chunks_ref[pl.ds(v * 4 + q, GROUPS, stride=TILES), half, :]
                for q in (2 * pair, 2 * pair + 1)
                for half in range(2)
            ]
            columns.append(jnp.concatenate(rows, 0))
        high, low = split(jnp.concatenate(columns, 1))
        high, low = split(dot(block_table, high) + dot(block_table, low))
        done = (dot(high, lane_table) + dot(low, lane_table)) * F32(2.0**-8)
        for v in range(4):
            mixed[v][pair * 256 : pair * 256 + 256, :] = done[:, v * 128 : v * 128 + 128]
    even = jnp.bitwise_and(lax.broadcasted_iota(jnp.int32, (8, 128), 0), 1) == 0

    def eight(group, carry):
        for inner in range(8):
            block = group * 8 + inner
            local_picks = chunks_ref[block * TILES + 16].astype(jnp.int32)
            sources = [mixed[v][pl.ds(block, 8, stride=GROUPS), :] for v in range(4)]
            found = []
            for part in range(2):
                local = jnp.broadcast_to(local_picks[part : part + 1, :], (8, 128))
                lane = jnp.bitwise_and(local, 127)
                vreg = jnp.bitwise_and(jnp.right_shift(local, 7), 3)
                got = None
                for v in range(4):
                    here = jnp.take_along_axis(sources[v], lane, axis=1)
                    got = here if got is None else jnp.where(vreg == v, here, got)
                found.append((got, jnp.right_shift(local, 9) == 1))
            (a, up_a), (b, up_b) = found
            picked = jnp.where(
                even,
                jnp.where(up_a, pltpu.roll(a, 7, 0), a),
                jnp.where(up_b, b, pltpu.roll(b, 1, 0)),
            )
            partner = group * 8 + (inner ^ 1)
            out_ref[pl.ds(pl.multiple_of(block * 16, 8), 8), :] = picked
            out_ref[pl.ds(pl.multiple_of(partner * 16 + 8, 8), 8), :] = picked
        return carry

    lax.fori_loop(0, GROUPS // 8, eight, 0)


def order_kernel(me_ref, got_ref, left_ref, sketch_ref, other_ref):
    mine = me_ref[0] * (16 * 32)
    for whose, target in enumerate((sketch_ref, other_ref)):
        for q in range(4):
            halves = []
            for part in range(2):
                place = whose * 8 + q * 2 + part
                halves.append(got_ref[pl.ds(place, GROUPS, stride=16), :])
                start = whose * 256 + part * 128
                left_ref[q * 32 : q * 32 + 32, start : start + 128] = got_ref[
                    pl.ds(mine + place, 32, stride=16), :
                ]
            target[:, q * GROUPS : (q + 1) * GROUPS] = jnp.concatenate(halves, 1).T


def gram_kernel(order, me_ref, sketch_ref, other_ref, *refs):
    parts, out_ref = refs[:-1], refs[-1]
    me = me_ref[0]
    right_high, right_low = split(jnp.concatenate([sketch_ref[...], other_ref[...]], 0))
    width = 128
    block = 0
    for part in parts:
        for piece in range(part.shape[0] // width):
            left_high, left_low = split(part[piece * width : (piece + 1) * width, :])
            product = dot(left_high, right_high) + dot(left_high, right_low) + dot(left_low, right_high)
            column = jnp.bitwise_xor(me, order[block])
            place = jnp.right_shift(column, 1) * 256 + jnp.bitwise_and(column, 1) * 64
            for q in range(4):
                start = pl.multiple_of(place + (q % 2) * 128 + (q // 2) * 32, 32)
                out_ref[pl.ds(start, 32), :] = product[q * 32 : q * 32 + 32]
            block += 1


def call(kernel, out_shape, scratch=(), **more):
    vmem = pl.BlockSpec(memory_space=pltpu.VMEM)
    many = isinstance(out_shape, (list, tuple))
    return pl.pallas_call(
        kernel,
        out_shape=out_shape,
        out_specs=[vmem] * len(out_shape) if many else vmem,
        scratch_shapes=list(scratch),
        compiler_params=pltpu.CompilerParams(vmem_limit_bytes=VMEM_LIMIT),
        **more,
    )


def shape(*dims):
    return jax.ShapeDtypeStruct(dims, F32)


def from_partner(x, axis, distance):
    return lax.ppermute(x, axis, [(i, i ^ distance) for i in range(lax.axis_size(axis))])


def shards(matrix, signs, picks):
    chunks = call(chunk_kernel, shape(GROUPS * TILES, 2, 128))(
        matrix, signs[None, :], picks.reshape(2, 128)
    )
    chunks = lax.all_to_all(chunks.reshape(GROUPS, TILES, 2, 128), "row", 0, 0, tiled=True)
    block_table = jnp.asarray(np.kron(np.eye(2), sylvester(2 * GROUPS)), BF16)
    lane_table = jnp.asarray(sylvester(LANES), BF16)
    picked = call(mix_kernel, shape(16 * GROUPS, 128), [pltpu.VMEM((8 * GROUPS, 128), F32)] * 4)(
        chunks.reshape(GROUPS * TILES, 2, 128), block_table, lane_table
    )
    picked = picked.reshape(GROUPS, 16, 128)
    picked = lax.all_to_all(picked, "row", 0, 0, tiled=True).reshape(16 * GROUPS, 128)

    vmem = pl.BlockSpec(memory_space=pltpu.VMEM)
    smem = pl.BlockSpec(memory_space=pltpu.SMEM)
    y_high = jnp.bitwise_and(lax.axis_index("row"), 1).astype(jnp.int32)[None]
    me = lax.axis_index("col").astype(jnp.int32)[None]
    left, sketch, other = call(
        order_kernel, [shape(128, 512), shape(256, 256), shape(256, 256)], in_specs=[smem, vmem]
    )(y_high, picked)

    pieces = [left]
    for distance in (4, 2, 1):
        held = pieces[0] if len(pieces) == 1 else jnp.concatenate(pieces, 0)
        pieces.append(from_partner(held, "col", distance))
    kernel = functools.partial(gram_kernel, (0, 4, 2, 6, 1, 5, 3, 7))
    gram = call(kernel, shape(1024, 256), in_specs=[smem] + [vmem] * 6)(me, sketch, other, *pieces)

    near = [[x * 16 + h * 4 + l * 2 + y for x in range(4) for l in range(2)] for h in range(4) for y in range(2)]
    far = [[x * 16 + h * 4 + l * 2 + y for h in range(4)] for x in range(4) for l in range(2) for y in range(2)]
    gram = lax.all_to_all(gram, "row", 0, 0, axis_index_groups=near, tiled=True)
    gram = jnp.sum(gram.reshape(8, 128, 256), 0)
    gram = lax.all_to_all(gram, "row", 0, 0, axis_index_groups=far, tiled=True)
    gram = jnp.sum(gram.reshape(4, 32, 256), 0) * F32(2.0**-14)
    return sketch, gram


def solution(mesh):
    placed = (P("row", "col"), P("row"), P("row"))
    return jax.shard_map(
        shards,
        mesh=mesh,
        in_specs=placed,
        out_specs=(P("row", "col"), P("row", "col")),
        check_vma=False,
    )
```

```python
import functools

import jax
import jax.numpy as jnp
import numpy as np
from jax import lax
from jax.experimental import pallas as pl
from jax.experimental.pallas import tpu as pltpu
from jax.sharding import PartitionSpec as P

F32 = jnp.float32
BF16 = jnp.bfloat16
GROUPS = 64
LANES = 512
TILES = 17
VMEM_LIMIT = 48 * 1024 * 1024


def sylvester(order):
    both = np.arange(order)[:, None] & np.arange(order)[None, :]
    parity = np.zeros_like(both)
    while both.any():
        parity ^= both & 1
        both >>= 1
    return (1 - 2 * parity).astype(np.float32)


def split(x):
    high = x.astype(BF16)
    return high, (x - high.astype(F32)).astype(BF16)


def dot(a, b):
    return jnp.dot(a, b, preferred_element_type=F32)


def chunk_kernel(matrix_ref, signs_ref, picks_ref, out_ref):
    signed = matrix_ref[...].T * signs_ref[...].astype(F32)
    for half in range(2):
        for v in range(4):
            start = half * LANES + v * 128
            for q in range(4):
                out_ref[pl.ds(v * 4 + q, GROUPS, stride=TILES), half, :] = signed[
                    q * GROUPS : (q + 1) * GROUPS, start : start + 128
                ]
    offsets = jnp.bitwise_and(picks_ref[...], 1023).astype(F32)
    for part in range(2):
        out_ref[pl.ds(16, GROUPS, stride=TILES), part, :] = jnp.broadcast_to(
            offsets[part : part + 1, :], (GROUPS, 128)
        )


def mix_kernel(chunks_ref, block_table_ref, lane_table_ref, out_ref, *mixed):
    block_table = block_table_ref[...]
    lane_table = lane_table_ref[...]
    for pair in range(2):
        columns = []
        for v in range(4):
            rows = [
                chunks_ref[pl.ds(v * 4 + q, GROUPS, stride=TILES), half, :]
                for q in (2 * pair, 2 * pair + 1)
                for half in range(2)
            ]
            columns.append(jnp.concatenate(rows, 0))
        high, low = split(jnp.concatenate(columns, 1))
        high, low = split(dot(block_table, high) + dot(block_table, low))
        done = (dot(high, lane_table) + dot(low, lane_table)) * F32(2.0**-8)
        for v in range(4):
            mixed[v][pair * 256 : pair * 256 + 256, :] = done[:, v * 128 : v * 128 + 128]
    even = jnp.bitwise_and(lax.broadcasted_iota(jnp.int32, (8, 128), 0), 1) == 0

    def eight(group, carry):
        for inner in range(8):
            block = group * 8 + inner
            local_picks = chunks_ref[block * TILES + 16].astype(jnp.int32)
            sources = [mixed[v][pl.ds(block, 8, stride=GROUPS), :] for v in range(4)]
            found = []
            for part in range(2):
                local = jnp.broadcast_to(local_picks[part : part + 1, :], (8, 128))
                lane = jnp.bitwise_and(local, 127)
                vreg = jnp.bitwise_and(jnp.right_shift(local, 7), 3)
                got = None
                for v in range(4):
                    here = jnp.take_along_axis(sources[v], lane, axis=1)
                    got = here if got is None else jnp.where(vreg == v, here, got)
                found.append((got, jnp.right_shift(local, 9) == 1))
            (a, up_a), (b, up_b) = found
            picked = jnp.where(
                even,
                jnp.where(up_a, pltpu.roll(a, 7, 0), a),
                jnp.where(up_b, b, pltpu.roll(b, 1, 0)),
            )
            partner = group * 8 + (inner ^ 1)
            out_ref[pl.ds(pl.multiple_of(block * 16, 8), 8), :] = picked
            out_ref[pl.ds(pl.multiple_of(partner * 16 + 8, 8), 8), :] = picked
        return carry

    lax.fori_loop(0, GROUPS // 8, eight, 0)


def order_kernel(y_high_ref, column_ref, got_ref, own_ref, up_ref, down_ref, far_ref, sketch_ref, other_ref):
    column = column_ref[0]
    ring = y_high_ref[0] * 4 + jnp.right_shift(column, 1)
    far = 2 + 4 * jnp.bitwise_and(column, 1)
    for step, target in ((0, own_ref), (1, up_ref), (7, down_ref), (far, far_ref)):
        y_high = jnp.right_shift(jnp.bitwise_and(ring + step, 7), 2)
        for whose in range(2):
            for q in range(4):
                for part in range(2):
                    place = jnp.bitwise_xor(y_high_ref[0], whose) * 8 + (y_high * (16 * 32) + q * 2 + part)
                    start = whose * 256 + part * 128
                    target[q * 32 : q * 32 + 32, start : start + 128] = got_ref[pl.ds(place, 32, stride=16), :]
    for whose, target in enumerate((sketch_ref, other_ref)):
        for q in range(4):
            halves = [got_ref[pl.ds(whose * 8 + q * 2 + part, GROUPS, stride=16), :] for part in range(2)]
            target[:, q * GROUPS : (q + 1) * GROUPS] = jnp.concatenate(halves, 1).T


def gram_kernel(y_high_ref, column_ref, sketch_ref, other_ref, *refs):
    parts, out_ref = refs[:-1], refs[-1]
    chip = jnp.right_shift(column_ref[0], 1)
    core = jnp.bitwise_and(column_ref[0], 1)
    first = y_high_ref[0] == 0
    sketch, other = sketch_ref[...], other_ref[...]
    right_high, right_low = split(
        jnp.concatenate([jnp.where(first, sketch, other), jnp.where(first, other, sketch)], 0)
    )
    for block, part in enumerate(parts):
        left_high, left_low = split(part[...])
        product = dot(left_high, right_high) + dot(left_high, right_low) + dot(left_low, right_high)
        chip_of = jnp.bitwise_and(chip + (0, 3, 1, 2)[block % 4], 3)
        core_of = jnp.bitwise_xor(core, block // 4)
        place = chip_of * 256 + core_of * 64
        for q in range(4):
            start = pl.multiple_of(place + (q % 2) * 128 + (q // 2) * 32, 32)
            out_ref[pl.ds(start, 32), :] = product[q * 32 : q * 32 + 32]


def call(kernel, out_shape, scratch=(), **more):
    vmem = pl.BlockSpec(memory_space=pltpu.VMEM)
    many = isinstance(out_shape, (list, tuple))
    return pl.pallas_call(
        kernel,
        out_shape=out_shape,
        out_specs=[vmem] * len(out_shape) if many else vmem,
        scratch_shapes=list(scratch),
        compiler_params=pltpu.CompilerParams(vmem_limit_bytes=VMEM_LIMIT),
        **more,
    )


def shape(*dims):
    return jax.ShapeDtypeStruct(dims, F32)


def from_partner(x, axis, distance):
    return lax.ppermute(x, axis, [(i, i ^ distance) for i in range(lax.axis_size(axis))])


def around_ring(x, steps):
    pairs = []
    for device in range(512):
        rest, ring, core = device // 16, device // 2 % 8, device % 2
        pairs.append((device, rest * 16 + (ring + steps[core]) % 8 * 2 + core))
    return lax.ppermute(x, ("row", "col"), pairs)


def shards(matrix, signs, picks):
    chunks = call(chunk_kernel, shape(GROUPS * TILES, 2, 128))(
        matrix, signs[None, :], picks.reshape(2, 128)
    )
    chunks = lax.all_to_all(chunks.reshape(GROUPS, TILES, 2, 128), "row", 0, 0, tiled=True)
    block_table = jnp.asarray(np.kron(np.eye(2), sylvester(2 * GROUPS)), BF16)
    lane_table = jnp.asarray(sylvester(LANES), BF16)
    picked = call(mix_kernel, shape(16 * GROUPS, 128), [pltpu.VMEM((8 * GROUPS, 128), F32)] * 4)(
        chunks.reshape(GROUPS * TILES, 2, 128), block_table, lane_table
    )
    picked = picked.reshape(GROUPS, 16, 128)
    picked = lax.all_to_all(picked, "row", 0, 0, tiled=True).reshape(16 * GROUPS, 128)

    vmem = pl.BlockSpec(memory_space=pltpu.VMEM)
    smem = pl.BlockSpec(memory_space=pltpu.SMEM)
    y_high = jnp.bitwise_and(lax.axis_index("row"), 1).astype(jnp.int32)[None]
    me = lax.axis_index("col").astype(jnp.int32)[None]
    own, up, down, far, sketch, other = call(
        order_kernel,
        [shape(128, 512)] * 4 + [shape(256, 256)] * 2,
        in_specs=[smem, smem, vmem],
    )(y_high, me, picked)
    pieces = [
        own,
        around_ring(up, (1, 1)),
        around_ring(down, (7, 7)),
        around_ring(far, (2, 6)),
    ]
    pieces += [from_partner(piece, "col", 1) for piece in pieces]
    gram = call(gram_kernel, shape(1024, 256), in_specs=[smem, smem] + [vmem] * 10)(
        y_high, me, sketch, other, *pieces
    )

    near = [[x * 16 + h * 4 + l * 2 + y for x in range(4) for l in range(2)] for h in range(4) for y in range(2)]
    far = [[x * 16 + h * 4 + l * 2 + y for h in range(4)] for x in range(4) for l in range(2) for y in range(2)]
    gram = lax.all_to_all(gram, "row", 0, 0, axis_index_groups=near, tiled=True)
    gram = jnp.sum(gram.reshape(8, 128, 256), 0)
    gram = lax.all_to_all(gram, "row", 0, 0, axis_index_groups=far, tiled=True)
    gram = jnp.sum(gram.reshape(4, 32, 256), 0) * F32(2.0**-14)
    return sketch, gram


def solution(mesh):
    placed = (P("row", "col"), P("row"), P("row"))
    return jax.shard_map(
        shards,
        mesh=mesh,
        in_specs=placed,
        out_specs=(P("row", "col"), P("row", "col")),
        check_vma=False,
    )
```

```python
import functools

import jax
import jax.numpy as jnp
import numpy as np
from jax import lax
from jax.experimental import pallas as pl
from jax.experimental.pallas import tpu as pltpu
from jax.sharding import PartitionSpec as P

F32 = jnp.float32
BF16 = jnp.bfloat16
GROUPS = 64
LANES = 512
TILES = 17
VMEM_LIMIT = 48 * 1024 * 1024


def sylvester(order):
    both = np.arange(order)[:, None] & np.arange(order)[None, :]
    parity = np.zeros_like(both)
    while both.any():
        parity ^= both & 1
        both >>= 1
    return (1 - 2 * parity).astype(np.float32)


def split(x):
    high = x.astype(BF16)
    return high, (x - high.astype(F32)).astype(BF16)


def dot(a, b):
    return jnp.dot(a, b, preferred_element_type=F32)


def chunk_kernel(matrix_ref, signs_ref, picks_ref, out_ref):
    signed = matrix_ref[...].T * signs_ref[...].astype(F32)
    for half in range(2):
        for v in range(4):
            start = half * LANES + v * 128
            for q in range(4):
                out_ref[pl.ds(v * 4 + q, GROUPS, stride=TILES), half, :] = signed[
                    q * GROUPS : (q + 1) * GROUPS, start : start + 128
                ]
    offsets = jnp.bitwise_and(picks_ref[...], 1023).astype(F32)
    for part in range(2):
        out_ref[pl.ds(16, GROUPS, stride=TILES), part, :] = jnp.broadcast_to(
            offsets[part : part + 1, :], (GROUPS, 128)
        )


def mix_kernel(chunks_ref, block_table_ref, lane_table_ref, out_ref, *mixed):
    block_table = block_table_ref[...]
    lane_table = lane_table_ref[...]
    for pair in range(2):
        columns = []
        for v in range(4):
            rows = [
                chunks_ref[pl.ds(v * 4 + q, GROUPS, stride=TILES), half, :]
                for q in (2 * pair, 2 * pair + 1)
                for half in range(2)
            ]
            columns.append(jnp.concatenate(rows, 0))
        high, low = split(jnp.concatenate(columns, 1))
        high, low = split(dot(block_table, high) + dot(block_table, low))
        done = (dot(high, lane_table) + dot(low, lane_table)) * F32(2.0**-8)
        for v in range(4):
            mixed[v][pair * 256 : pair * 256 + 256, :] = done[:, v * 128 : v * 128 + 128]
    even = jnp.bitwise_and(lax.broadcasted_iota(jnp.int32, (8, 128), 0), 1) == 0

    def eight(group, carry):
        for inner in range(8):
            block = group * 8 + inner
            local_picks = chunks_ref[block * TILES + 16].astype(jnp.int32)
            sources = [mixed[v][pl.ds(block, 8, stride=GROUPS), :] for v in range(4)]
            found = []
            for part in range(2):
                local = jnp.broadcast_to(local_picks[part : part + 1, :], (8, 128))
                lane = jnp.bitwise_and(local, 127)
                vreg = jnp.bitwise_and(jnp.right_shift(local, 7), 3)
                got = None
                for v in range(4):
                    here = jnp.take_along_axis(sources[v], lane, axis=1)
                    got = here if got is None else jnp.where(vreg == v, here, got)
                found.append((got, jnp.right_shift(local, 9) == 1))
            (a, up_a), (b, up_b) = found
            picked = jnp.where(
                even,
                jnp.where(up_a, pltpu.roll(a, 7, 0), a),
                jnp.where(up_b, b, pltpu.roll(b, 1, 0)),
            )
            partner = group * 8 + (inner ^ 1)
            out_ref[pl.ds(pl.multiple_of(block * 16, 8), 8), :] = picked
            out_ref[pl.ds(pl.multiple_of(partner * 16 + 8, 8), 8), :] = picked
        return carry

    lax.fori_loop(0, GROUPS // 8, eight, 0)


def half_columns(y_high_ref, column_ref, got_ref, steps, targets):
    ring = y_high_ref[0] * 4 + jnp.right_shift(column_ref[0], 1)
    for step, target in zip(steps, targets):
        y_high = jnp.right_shift(jnp.bitwise_and(ring + step, 7), 2)
        for whose in range(2):
            for q in range(4):
                for part in range(2):
                    place = jnp.bitwise_xor(y_high_ref[0], whose) * 8 + (y_high * (16 * 32) + q * 2 + part)
                    start = whose * 256 + part * 128
                    target[q * 32 : q * 32 + 32, start : start + 128] = got_ref[pl.ds(place, 32, stride=16), :]


def far_kernel(y_high_ref, column_ref, got_ref, far_ref):
    step = 2 + 4 * jnp.bitwise_and(column_ref[0], 1)
    half_columns(y_high_ref, column_ref, got_ref, (step,), (far_ref,))


def order_kernel(y_high_ref, column_ref, got_ref, own_ref, up_ref, down_ref, sketch_ref, right_ref):
    half_columns(y_high_ref, column_ref, got_ref, (0, 1, 7), (own_ref, up_ref, down_ref))
    for whose in range(2):
        columns = []
        for q in range(4):
            halves = [got_ref[pl.ds(whose * 8 + q * 2 + part, GROUPS, stride=16), :] for part in range(2)]
            columns.append(jnp.concatenate(halves, 1))
        rows = jnp.concatenate(columns, 0).T
        start = pl.multiple_of(jnp.bitwise_xor(y_high_ref[0], whose) * 256, 256)
        right_ref[pl.ds(start, 256), :] = rows
        if whose == 0:
            sketch_ref[...] = rows


CHIPS_ON = (0, 2, 3, 1)


def gram_kernel(column_ref, right_ref, *refs):
    out_ref = refs[-1]
    parts = [ref.at[i : i + 128] for ref in refs[:-1] for i in range(0, ref.shape[0], 128)]
    chip = jnp.right_shift(column_ref[0], 1)
    core = jnp.bitwise_and(column_ref[0], 1)
    right_high, right_low = split(right_ref[...])
    for block, part in enumerate(parts):
        left_high, left_low = split(part[...])
        product = dot(left_high, right_high) + dot(left_high, right_low) + dot(left_low, right_high)
        chip_of = jnp.bitwise_and(chip + CHIPS_ON[block % 4], 3)
        core_of = jnp.bitwise_xor(core, block // 4)
        place = chip_of * 256 + core_of * 64
        for q in range(4):
            start = pl.multiple_of(place + (q % 2) * 128 + (q // 2) * 32, 32)
            out_ref[pl.ds(start, 32), :] = product[q * 32 : q * 32 + 32]


def call(kernel, out_shape, scratch=(), **more):
    vmem = pl.BlockSpec(memory_space=pltpu.VMEM)
    many = isinstance(out_shape, (list, tuple))
    return pl.pallas_call(
        kernel,
        out_shape=out_shape,
        out_specs=[vmem] * len(out_shape) if many else vmem,
        scratch_shapes=list(scratch),
        compiler_params=pltpu.CompilerParams(vmem_limit_bytes=VMEM_LIMIT),
        **more,
    )


def shape(*dims):
    return jax.ShapeDtypeStruct(dims, F32)


def from_partner(x, axis, distance):
    return lax.ppermute(x, axis, [(i, i ^ distance) for i in range(lax.axis_size(axis))])


def around_ring(x, steps):
    pairs = []
    for device in range(512):
        rest, ring, core = device // 16, device // 2 % 8, device % 2
        pairs.append((device, rest * 16 + (ring + steps[core]) % 8 * 2 + core))
    return lax.ppermute(x, ("row", "col"), pairs)


def shards(matrix, signs, picks):
    chunks = call(chunk_kernel, shape(GROUPS * TILES, 2, 128))(
        matrix, signs[None, :], picks.reshape(2, 128)
    )
    chunks = lax.all_to_all(chunks.reshape(GROUPS, TILES, 2, 128), "row", 0, 0, tiled=True)
    block_table = jnp.asarray(np.kron(np.eye(2), sylvester(2 * GROUPS)), BF16)
    lane_table = jnp.asarray(sylvester(LANES), BF16)
    picked = call(mix_kernel, shape(16 * GROUPS, 128), [pltpu.VMEM((8 * GROUPS, 128), F32)] * 4)(
        chunks.reshape(GROUPS * TILES, 2, 128), block_table, lane_table
    )
    picked = picked.reshape(GROUPS, 16, 128)
    picked = lax.all_to_all(picked, "row", 0, 0, tiled=True).reshape(16 * GROUPS, 128)

    vmem = pl.BlockSpec(memory_space=pltpu.VMEM)
    smem = pl.BlockSpec(memory_space=pltpu.SMEM)
    y_high = jnp.bitwise_and(lax.axis_index("row"), 1).astype(jnp.int32)[None]
    me = lax.axis_index("col").astype(jnp.int32)[None]
    places = [smem, smem, vmem]
    far = call(far_kernel, shape(128, 512), in_specs=places)(y_high, me, picked)
    far = around_ring(far, (2, 6))
    own, up, down, sketch, right = call(
        order_kernel,
        [shape(128, 512)] * 3 + [shape(256, 256), shape(512, 256)],
        in_specs=places,
    )(y_high, me, picked)
    sides = [around_ring(up, (1, 1)), around_ring(down, (7, 7))]
    pieces = [own, far, *sides]
    pieces += [from_partner(jnp.concatenate(pair, 0), "col", 1) for pair in ((own, far), sides)]
    gram = call(gram_kernel, shape(1024, 256), in_specs=[smem] + [vmem] * 7)(me, right, *pieces)

    near = [[x * 16 + h * 4 + l * 2 + y for x in range(4) for l in range(2)] for h in range(4) for y in range(2)]
    far = [[x * 16 + h * 4 + l * 2 + y for h in range(4)] for x in range(4) for l in range(2) for y in range(2)]
    gram = lax.all_to_all(gram, "row", 0, 0, axis_index_groups=near, tiled=True)
    gram = jnp.sum(gram.reshape(8, 128, 256), 0)
    gram = lax.all_to_all(gram, "row", 0, 0, axis_index_groups=far, tiled=True)
    gram = jnp.sum(gram.reshape(4, 32, 256), 0) * F32(2.0**-14)
    return sketch, gram


def solution(mesh):
    placed = (P("row", "col"), P("row"), P("row"))
    return jax.shard_map(
        shards,
        mesh=mesh,
        in_specs=placed,
        out_specs=(P("row", "col"), P("row", "col")),
        check_vma=False,
    )
```

```python
import functools

import jax
import jax.numpy as jnp
import numpy as np
from jax import lax
from jax.experimental import pallas as pl
from jax.experimental.pallas import tpu as pltpu
from jax.sharding import PartitionSpec as P

F32 = jnp.float32
BF16 = jnp.bfloat16
GROUPS = 64
LANES = 512
TILES = 17
VMEM_LIMIT = 48 * 1024 * 1024


def sylvester(order):
    both = np.arange(order)[:, None] & np.arange(order)[None, :]
    parity = np.zeros_like(both)
    while both.any():
        parity ^= both & 1
        both >>= 1
    return (1 - 2 * parity).astype(np.float32)


def split(x):
    high = x.astype(BF16)
    return high, (x - high.astype(F32)).astype(BF16)


def dot(a, b):
    return jnp.dot(a, b, preferred_element_type=F32)


def chunk_kernel(matrix_ref, signs_ref, picks_ref, out_ref):
    signed = matrix_ref[...].T * signs_ref[...].astype(F32)
    for half in range(2):
        for v in range(4):
            start = half * LANES + v * 128
            for q in range(4):
                out_ref[pl.ds(v * 4 + q, GROUPS, stride=TILES), half, :] = signed[
                    q * GROUPS : (q + 1) * GROUPS, start : start + 128
                ]
    offsets = jnp.bitwise_and(picks_ref[...], 1023).astype(F32)
    for part in range(2):
        out_ref[pl.ds(16, GROUPS, stride=TILES), part, :] = jnp.broadcast_to(
            offsets[part : part + 1, :], (GROUPS, 128)
        )


def mix_kernel(chunks_ref, block_table_ref, lane_table_ref, out_ref, *mixed):
    block_table = block_table_ref[...]
    lane_table = lane_table_ref[...]
    for pair in range(2):
        columns = []
        for v in range(4):
            rows = [
                chunks_ref[pl.ds(v * 4 + q, GROUPS, stride=TILES), half, :]
                for q in (2 * pair, 2 * pair + 1)
                for half in range(2)
            ]
            columns.append(jnp.concatenate(rows, 0))
        high, low = split(jnp.concatenate(columns, 1))
        high, low = split(dot(block_table, high) + dot(block_table, low))
        done = (dot(high, lane_table) + dot(low, lane_table)) * F32(2.0**-8)
        for v in range(4):
            mixed[v][pair * 256 : pair * 256 + 256, :] = done[:, v * 128 : v * 128 + 128]
    even = jnp.bitwise_and(lax.broadcasted_iota(jnp.int32, (8, 128), 0), 1) == 0

    def eight(group, carry):
        for inner in range(8):
            block = group * 8 + inner
            local_picks = chunks_ref[block * TILES + 16].astype(jnp.int32)
            sources = [mixed[v][pl.ds(block, 8, stride=GROUPS), :] for v in range(4)]
            found = []
            for part in range(2):
                local = jnp.broadcast_to(local_picks[part : part + 1, :], (8, 128))
                lane = jnp.bitwise_and(local, 127)
                vreg = jnp.bitwise_and(jnp.right_shift(local, 7), 3)
                got = None
                for v in range(4):
                    here = jnp.take_along_axis(sources[v], lane, axis=1)
                    got = here if got is None else jnp.where(vreg == v, here, got)
                found.append((got, jnp.right_shift(local, 9) == 1))
            (a, up_a), (b, up_b) = found
            picked = jnp.where(
                even,
                jnp.where(up_a, pltpu.roll(a, 7, 0), a),
                jnp.where(up_b, b, pltpu.roll(b, 1, 0)),
            )
            partner = group * 8 + (inner ^ 1)
            out_ref[pl.ds(block * 16, 8), :] = picked
            out_ref[pl.ds(partner * 16 + 8, 8), :] = picked
        return carry

    for group in range(GROUPS // 8):
        eight(group, 0)


def half_columns(y_high_ref, column_ref, got_ref, steps, targets):
    ring = y_high_ref[0] * 4 + jnp.right_shift(column_ref[0], 1)
    for step, target in zip(steps, targets):
        y_high = jnp.right_shift(jnp.bitwise_and(ring + step, 7), 2)
        for whose in range(2):
            for q in range(4):
                for part in range(2):
                    place = jnp.bitwise_xor(y_high_ref[0], whose) * 8 + (y_high * (16 * 32) + q * 2 + part)
                    start = whose * 256 + part * 128
                    target[q * 32 : q * 32 + 32, start : start + 128] = got_ref[pl.ds(place, 32, stride=16), :]


def far_kernel(y_high_ref, column_ref, got_ref, far_ref):
    step = 2 + 4 * jnp.bitwise_and(column_ref[0], 1)
    half_columns(y_high_ref, column_ref, got_ref, (step,), (far_ref,))


def near_kernel(y_high_ref, column_ref, got_ref, own_ref, up_ref, down_ref):
    half_columns(y_high_ref, column_ref, got_ref, (0, 1, 7), (own_ref, up_ref, down_ref))


def order_kernel(y_high_ref, got_ref, sketch_ref, right_ref):
    for whose in range(2):
        columns = []
        for q in range(4):
            halves = [got_ref[pl.ds(whose * 8 + q * 2 + part, GROUPS, stride=16), :] for part in range(2)]
            columns.append(jnp.concatenate(halves, 1))
        rows = jnp.concatenate(columns, 0).T
        start = pl.multiple_of(jnp.bitwise_xor(y_high_ref[0], whose) * 256, 256)
        right_ref[pl.ds(start, 256), :] = rows
        if whose == 0:
            sketch_ref[...] = rows


CHIPS_ON = (0, 2, 3, 1)


def gram_kernel(column_ref, right_ref, *refs):
    out_ref = refs[-1]
    parts = [ref.at[i : i + 128] for ref in refs[:-1] for i in range(0, ref.shape[0], 128)]
    chip = jnp.right_shift(column_ref[0], 1)
    core = jnp.bitwise_and(column_ref[0], 1)
    right_high, right_low = split(right_ref[...])
    for block, part in enumerate(parts):
        left_high, left_low = split(part[...])
        product = dot(left_high, right_high) + dot(left_high, right_low) + dot(left_low, right_high)
        chip_of = jnp.bitwise_and(chip + CHIPS_ON[block % 4], 3)
        core_of = jnp.bitwise_xor(core, block // 4)
        place = chip_of * 256 + core_of * 64
        for q in range(4):
            start = pl.multiple_of(place + (q % 2) * 128 + (q // 2) * 32, 32)
            out_ref[pl.ds(start, 32), :] = product[q * 32 : q * 32 + 32] * F32(2.0**-14)


def call(kernel, out_shape, scratch=(), **more):
    vmem = pl.BlockSpec(memory_space=pltpu.VMEM)
    many = isinstance(out_shape, (list, tuple))
    return pl.pallas_call(
        kernel,
        out_shape=out_shape,
        out_specs=[vmem] * len(out_shape) if many else vmem,
        scratch_shapes=list(scratch),
        compiler_params=pltpu.CompilerParams(vmem_limit_bytes=VMEM_LIMIT),
        **more,
    )


def shape(*dims):
    return jax.ShapeDtypeStruct(dims, F32)


def from_partner(x, axis, distance):
    return lax.ppermute(x, axis, [(i, i ^ distance) for i in range(lax.axis_size(axis))])


def around_ring(x, steps):
    pairs = []
    for device in range(512):
        rest, ring, core = device // 16, device // 2 % 8, device % 2
        pairs.append((device, rest * 16 + (ring + steps[core]) % 8 * 2 + core))
    return lax.ppermute(x, ("row", "col"), pairs)


def shards(matrix, signs, picks):
    chunks = call(chunk_kernel, shape(GROUPS * TILES, 2, 128))(
        matrix, signs[None, :], picks.reshape(2, 128)
    )
    chunks = lax.all_to_all(chunks.reshape(GROUPS, TILES, 2, 128), "row", 0, 0, tiled=True)
    block_table = jnp.asarray(np.kron(np.eye(2), sylvester(2 * GROUPS)), BF16)
    lane_table = jnp.asarray(sylvester(LANES), BF16)
    picked = call(mix_kernel, shape(16 * GROUPS, 128), [pltpu.VMEM((8 * GROUPS, 128), F32)] * 4)(
        chunks.reshape(GROUPS * TILES, 2, 128), block_table, lane_table
    )
    picked = picked.reshape(GROUPS, 16, 128)
    picked = lax.all_to_all(picked, "row", 0, 0, tiled=True).reshape(16 * GROUPS, 128)

    vmem = pl.BlockSpec(memory_space=pltpu.VMEM)
    smem = pl.BlockSpec(memory_space=pltpu.SMEM)
    y_high = jnp.bitwise_and(lax.axis_index("row"), 1).astype(jnp.int32)[None]
    me = lax.axis_index("col").astype(jnp.int32)[None]
    places = [smem, smem, vmem]
    far = call(far_kernel, shape(128, 512), in_specs=places)(y_high, me, picked)
    far = around_ring(far, (2, 6))
    own, up, down = call(near_kernel, [shape(128, 512)] * 3, in_specs=places)(y_high, me, picked)
    sketch, right = call(order_kernel, [shape(256, 256), shape(512, 256)], in_specs=[smem, vmem])(
        y_high, picked
    )
    sides = [around_ring(up, (1, 1)), around_ring(down, (7, 7))]
    pieces = [own, far, *sides]
    pieces += [from_partner(jnp.concatenate(pair, 0), "col", 1) for pair in ((own, far), sides)]
    gram = call(gram_kernel, shape(1024, 256), in_specs=[smem] + [vmem] * 7)(me, right, *pieces)

    near = [[x * 16 + h * 4 + l * 2 + y for x in range(4) for l in range(2)] for h in range(4) for y in range(2)]
    far = [[x * 16 + h * 4 + l * 2 + y for h in range(4)] for x in range(4) for l in range(2) for y in range(2)]
    gram = lax.all_to_all(gram, "row", 0, 0, axis_index_groups=near, tiled=True)
    gram = jnp.sum(gram.reshape(8, 128, 256), 0)
    gram = lax.all_to_all(gram, "row", 0, 0, axis_index_groups=far, tiled=True)
    gram = jnp.sum(gram.reshape(4, 32, 256), 0)
    return sketch, gram


def solution(mesh):
    placed = (P("row", "col"), P("row"), P("row"))
    return jax.shard_map(
        shards,
        mesh=mesh,
        in_specs=placed,
        out_specs=(P("row", "col"), P("row", "col")),
        check_vma=False,
    )
```

```python
import functools

import jax
import jax.numpy as jnp
import numpy as np
from jax import lax
from jax.experimental import pallas as pl
from jax.experimental.pallas import tpu as pltpu
from jax.sharding import PartitionSpec as P

F32 = jnp.float32
BF16 = jnp.bfloat16
GROUPS = 64
LANES = 512
TILES = 17
VMEM_LIMIT = 48 * 1024 * 1024


def sylvester(order):
    both = np.arange(order)[:, None] & np.arange(order)[None, :]
    parity = np.zeros_like(both)
    while both.any():
        parity ^= both & 1
        both >>= 1
    return (1 - 2 * parity).astype(np.float32)


def split(x):
    high = x.astype(BF16)
    return high, (x - high.astype(F32)).astype(BF16)


def dot(a, b):
    return jnp.dot(a, b, preferred_element_type=F32)


def chunk_kernel(matrix_ref, signs_ref, picks_ref, out_ref):
    signed = matrix_ref[...].T * signs_ref[...].astype(F32)
    for half in range(2):
        for v in range(4):
            start = half * LANES + v * 128
            for q in range(4):
                out_ref[pl.ds(v * 4 + q, GROUPS, stride=TILES), half, :] = signed[
                    q * GROUPS : (q + 1) * GROUPS, start : start + 128
                ]
    offsets = jnp.bitwise_and(picks_ref[...], 1023).astype(F32)
    for part in range(2):
        out_ref[pl.ds(16, GROUPS, stride=TILES), part, :] = jnp.broadcast_to(
            offsets[part : part + 1, :], (GROUPS, 128)
        )


def mix_kernel(chunks_ref, block_table_ref, lane_table_ref, out_ref, *mixed):
    block_table = block_table_ref[...]
    lane_table = lane_table_ref[...]
    for pair in range(2):
        columns = []
        for v in range(4):
            rows = [
                chunks_ref[pl.ds(v * 4 + q, GROUPS, stride=TILES), half, :]
                for q in (2 * pair, 2 * pair + 1)
                for half in range(2)
            ]
            columns.append(jnp.concatenate(rows, 0))
        high, low = split(jnp.concatenate(columns, 1))
        high, low = split(dot(block_table, high) + dot(block_table, low))
        done = (dot(high, lane_table) + dot(low, lane_table)) * F32(2.0**-8)
        for v in range(4):
            mixed[v][pair * 256 : pair * 256 + 256, :] = done[:, v * 128 : v * 128 + 128]
    even = jnp.bitwise_and(lax.broadcasted_iota(jnp.int32, (8, 128), 0), 1) == 0

    def eight(group, carry):
        for inner in range(8):
            block = group * 8 + inner
            local_picks = chunks_ref[block * TILES + 16].astype(jnp.int32)
            sources = [mixed[v][pl.ds(block, 8, stride=GROUPS), :] for v in range(4)]
            found = []
            for part in range(2):
                local = jnp.broadcast_to(local_picks[part : part + 1, :], (8, 128))
                lane = jnp.bitwise_and(local, 127)
                vreg = jnp.bitwise_and(jnp.right_shift(local, 7), 3)
                got = None
                for v in range(4):
                    here = jnp.take_along_axis(sources[v], lane, axis=1)
                    got = here if got is None else jnp.where(vreg == v, here, got)
                found.append((got, jnp.right_shift(local, 9) == 1))
            (a, up_a), (b, up_b) = found
            picked = jnp.where(
                even,
                jnp.where(up_a, pltpu.roll(a, 7, 0), a),
                jnp.where(up_b, b, pltpu.roll(b, 1, 0)),
            )
            partner = group * 8 + (inner ^ 1)
            out_ref[pl.ds(block * 16, 8), :] = picked
            out_ref[pl.ds(partner * 16 + 8, 8), :] = picked
        return carry

    for group in range(GROUPS // 8):
        eight(group, 0)


def half_columns(y_high_ref, column_ref, got_ref, steps, targets):
    ring = y_high_ref[0] * 4 + jnp.right_shift(column_ref[0], 1)
    for step, target in zip(steps, targets):
        y_high = jnp.right_shift(jnp.bitwise_and(ring + step, 7), 2)
        for whose in range(2):
            for q in range(4):
                for part in range(2):
                    place = jnp.bitwise_xor(y_high_ref[0], whose) * 8 + (y_high * (16 * 32) + q * 2 + part)
                    start = whose * 256 + part * 128
                    target[q * 32 : q * 32 + 32, start : start + 128] = got_ref[pl.ds(place, 32, stride=16), :]


def far_kernel(y_high_ref, column_ref, got_ref, far_ref):
    step = 2 + 4 * jnp.bitwise_and(column_ref[0], 1)
    half_columns(y_high_ref, column_ref, got_ref, (step,), (far_ref,))


def near_kernel(y_high_ref, column_ref, got_ref, after_ref, own_ref, up_ref, down_ref):
    half_columns(y_high_ref, column_ref, got_ref, (0, 1, 7), (own_ref, up_ref, down_ref))


def order_kernel(y_high_ref, got_ref, after_ref, sketch_ref, right_ref, right_too_ref):
    rows = []
    for whose in range(2):
        columns = []
        for q in range(4):
            halves = [got_ref[pl.ds(whose * 8 + q * 2 + part, GROUPS, stride=16), :] for part in range(2)]
            columns.append(jnp.concatenate(halves, 1))
        rows.append(jnp.concatenate(columns, 0).T)
    sketch_ref[...] = rows[0]
    first = y_high_ref[0] == 0
    right_ref[...] = jnp.where(first, rows[0], rows[1])
    right_too_ref[...] = jnp.where(first, rows[1], rows[0])


def products(lefts, rights):
    right_high, right_low = split(jnp.concatenate([right[...] for right in rights], 0))
    for block, left in enumerate(lefts):
        left_high, left_low = split(left[...])
        product = dot(left_high, right_high) + dot(left_high, right_low) + dot(left_low, right_high)
        yield block, product * F32(2.0**-14)


def half_gram_kernel(own_ref, far_ref, up_ref, down_ref, right_ref, right_too_ref, out_ref):
    for block, product in products((own_ref, far_ref, up_ref, down_ref), (right_ref, right_too_ref)):
        out_ref[block * 128 : block * 128 + 128, :] = product


def gram_kernel(column_ref, half_ref, own_ref, far_ref, up_ref, down_ref, right_ref, right_too_ref, out_ref):
    chip = jnp.right_shift(column_ref[0], 1)
    core = jnp.bitwise_and(column_ref[0], 1)
    for block, product in products((own_ref, far_ref, up_ref, down_ref), (right_ref, right_too_ref)):
        place = jnp.bitwise_and(chip + (0, 2, 3, 1)[block], 3) * 256
        for q in range(4):
            start = place + (q % 2) * 128 + (q // 2) * 32
            mine = pl.multiple_of(start + core * 64, 32)
            out_ref[pl.ds(mine, 32), :] = half_ref[block * 128 + q * 32 : block * 128 + q * 32 + 32, :]
            others = pl.multiple_of(start + (1 - core) * 64, 32)
            out_ref[pl.ds(others, 32), :] = product[q * 32 : q * 32 + 32]


def call(kernel, out_shape, scratch=(), **more):
    vmem = pl.BlockSpec(memory_space=pltpu.VMEM)
    many = isinstance(out_shape, (list, tuple))
    return pl.pallas_call(
        kernel,
        out_shape=out_shape,
        out_specs=[vmem] * len(out_shape) if many else vmem,
        scratch_shapes=list(scratch),
        compiler_params=pltpu.CompilerParams(vmem_limit_bytes=VMEM_LIMIT),
        **more,
    )


def shape(*dims):
    return jax.ShapeDtypeStruct(dims, F32)


def from_partner(x, axis, distance):
    return lax.ppermute(x, axis, [(i, i ^ distance) for i in range(lax.axis_size(axis))])


def around_ring(x, steps):
    pairs = []
    for device in range(512):
        rest, ring, core = device // 16, device // 2 % 8, device % 2
        pairs.append((device, rest * 16 + (ring + steps[core]) % 8 * 2 + core))
    return lax.ppermute(x, ("row", "col"), pairs)


def shards(matrix, signs, picks):
    chunks = call(chunk_kernel, shape(GROUPS * TILES, 2, 128))(
        matrix, signs[None, :], picks.reshape(2, 128)
    )
    chunks = lax.all_to_all(chunks.reshape(GROUPS, TILES, 2, 128), "row", 0, 0, tiled=True)
    block_table = jnp.asarray(np.kron(np.eye(2), sylvester(2 * GROUPS)), BF16)
    lane_table = jnp.asarray(sylvester(LANES), BF16)
    picked = call(mix_kernel, shape(16 * GROUPS, 128), [pltpu.VMEM((8 * GROUPS, 128), F32)] * 4)(
        chunks.reshape(GROUPS * TILES, 2, 128), block_table, lane_table
    )
    picked = picked.reshape(GROUPS, 16, 128)
    picked = lax.all_to_all(picked, "row", 0, 0, tiled=True).reshape(16 * GROUPS, 128)

    vmem = pl.BlockSpec(memory_space=pltpu.VMEM)
    smem = pl.BlockSpec(memory_space=pltpu.SMEM)
    y_high = jnp.bitwise_and(lax.axis_index("row"), 1).astype(jnp.int32)[None]
    me = lax.axis_index("col").astype(jnp.int32)[None]
    places = [smem, smem, vmem]
    after = pl.BlockSpec(memory_space=pl.ANY)
    far_left = call(far_kernel, shape(128, 512), in_specs=places)(y_high, me, picked)
    far = around_ring(far_left, (2, 6))
    own, up, down = call(near_kernel, [shape(128, 512)] * 3, in_specs=[*places, after])(
        y_high, me, picked, far_left
    )
    sketch, *right = call(
        order_kernel, [shape(256, 256)] * 3, in_specs=[smem, vmem, after]
    )(y_high, picked, own)
    up, down = around_ring(up, (1, 1)), around_ring(down, (7, 7))
    other = [from_partner(part, "col", 1) for part in right]
    half = call(
        half_gram_kernel,
        shape(512, 256),
        cost_estimate=pl.CostEstimate(flops=6 * 512 * 512 * 256, bytes_accessed=2 << 20, transcendentals=0),
    )(own, far, up, down, *right)
    gram = call(gram_kernel, shape(1024, 256), in_specs=[smem] + [vmem] * 7)(
        me, half, own, far, up, down, *other
    )

    near = [
        [(x * 16 + h * 4 + l * 2 + y) * 8 + c * 2 + core for x in range(4) for l in range(2) for core in range(2)]
        for h in range(4)
        for y in range(2)
        for c in range(4)
    ]
    far = [[x * 16 + h * 4 + l * 2 + y for h in range(4)] for x in range(4) for l in range(2) for y in range(2)]
    gram = lax.all_to_all(gram, ("row", "col"), 0, 0, axis_index_groups=near, tiled=True)
    gram = jnp.sum(gram.reshape(8, 2, 64, 256), 0).reshape(128, 256)
    gram = lax.all_to_all(gram, "row", 0, 0, axis_index_groups=far, tiled=True)
    gram = jnp.sum(gram.reshape(4, 32, 256), 0)
    return sketch, gram


def solution(mesh):
    placed = (P("row", "col"), P("row"), P("row"))
    return jax.shard_map(
        shards,
        mesh=mesh,
        in_specs=placed,
        out_specs=(P("row", "col"), P("row", "col")),
        check_vma=False,
    )
```

```python
import functools

import jax
import jax.numpy as jnp
import numpy as np
from jax import lax
from jax.experimental import pallas as pl
from jax.experimental.pallas import tpu as pltpu
from jax.sharding import PartitionSpec as P

F32 = jnp.float32
BF16 = jnp.bfloat16
GROUPS = 64
LANES = 512
TILES = 17
VMEM_LIMIT = 48 * 1024 * 1024


def sylvester(order):
    both = np.arange(order)[:, None] & np.arange(order)[None, :]
    parity = np.zeros_like(both)
    while both.any():
        parity ^= both & 1
        both >>= 1
    return (1 - 2 * parity).astype(np.float32)


def split(x):
    high = x.astype(BF16)
    return high, (x - high.astype(F32)).astype(BF16)


def dot(a, b):
    return jnp.dot(a, b, preferred_element_type=F32)


def chunk_kernel(matrix_ref, signs_ref, picks_ref, out_ref):
    signed = matrix_ref[...].T * signs_ref[...].astype(F32)
    for half in range(2):
        for v in range(4):
            start = half * LANES + v * 128
            for q in range(4):
                out_ref[pl.ds(v * 4 + q, GROUPS, stride=TILES), half, :] = signed[
                    q * GROUPS : (q + 1) * GROUPS, start : start + 128
                ]
    offsets = jnp.bitwise_and(picks_ref[...], 1023).astype(F32)
    for part in range(2):
        out_ref[pl.ds(16, GROUPS, stride=TILES), part, :] = jnp.broadcast_to(
            offsets[part : part + 1, :], (GROUPS, 128)
        )


def mix_kernel(chunks_ref, block_table_ref, lane_table_ref, out_ref, mixed):
    columns = []
    for v in range(4):
        rows = [
            chunks_ref[pl.ds(v * 4 + q, GROUPS, stride=TILES), half, :] for q in range(4) for half in range(2)
        ]
        columns.append(jnp.concatenate(rows, 0))
    high, low = split(jnp.concatenate(columns, 1))
    block_table = block_table_ref[...]
    high, low = split(dot(block_table, high) + dot(block_table, low))
    lane_table = lane_table_ref[...]
    mixed[...] = (dot(high, lane_table) + dot(low, lane_table)) * F32(2.0**-8)
    even = jnp.bitwise_and(lax.broadcasted_iota(jnp.int32, (8, 128), 0), 1) == 0

    def eight(group, carry):
        for inner in range(8):
            block = group * 8 + inner
            local_picks = chunks_ref[block * TILES + 16].astype(jnp.int32)
            sources = [mixed[block * 8 : block * 8 + 8, v * 128 : v * 128 + 128] for v in range(4)]
            found = []
            for part in range(2):
                local = jnp.broadcast_to(local_picks[part : part + 1, :], (8, 128))
                lane = jnp.bitwise_and(local, 127)
                vreg = jnp.bitwise_and(jnp.right_shift(local, 7), 3)
                got = None
                for v in range(4):
                    here = jnp.take_along_axis(sources[v], lane, axis=1)
                    got = here if got is None else jnp.where(vreg == v, here, got)
                found.append((got, jnp.right_shift(local, 9) == 1))
            (a, up_a), (b, up_b) = found
            picked = jnp.where(
                even,
                jnp.where(up_a, pltpu.roll(a, 7, 0), a),
                jnp.where(up_b, b, pltpu.roll(b, 1, 0)),
            )
            partner = group * 8 + (inner ^ 1)
            out_ref[pl.ds(block * 16, 8), :] = picked
            out_ref[pl.ds(partner * 16 + 8, 8), :] = picked
        return carry

    for group in range(GROUPS // 8):
        eight(group, 0)


def half_columns(y_high_ref, column_ref, got_ref, steps, targets):
    ring = y_high_ref[0] * 4 + jnp.right_shift(column_ref[0], 1)
    for step, target in zip(steps, targets):
        y_high = jnp.right_shift(jnp.bitwise_and(ring + step, 7), 2)
        for whose in range(2):
            for q in range(4):
                for part in range(2):
                    place = jnp.bitwise_xor(y_high_ref[0], whose) * 8 + (y_high * (16 * 32) + q * 2 + part)
                    start = whose * 256 + part * 128
                    target[q * 32 : q * 32 + 32, start : start + 128] = got_ref[pl.ds(place, 32, stride=16), :]


def far_kernel(y_high_ref, column_ref, got_ref, far_ref):
    step = 2 + 4 * jnp.bitwise_and(column_ref[0], 1)
    half_columns(y_high_ref, column_ref, got_ref, (step,), (far_ref,))


def near_kernel(y_high_ref, column_ref, got_ref, after_ref, own_ref, up_ref, down_ref):
    half_columns(y_high_ref, column_ref, got_ref, (0, 1, 7), (own_ref, up_ref, down_ref))


def order_kernel(y_high_ref, got_ref, after_ref, sketch_ref, right_ref, right_too_ref):
    rows = []
    for whose in range(2):
        columns = []
        for q in range(4):
            halves = [got_ref[pl.ds(whose * 8 + q * 2 + part, GROUPS, stride=16), :] for part in range(2)]
            columns.append(jnp.concatenate(halves, 1))
        rows.append(jnp.concatenate(columns, 0).T)
    sketch_ref[...] = rows[0]
    first = y_high_ref[0] == 0
    right_ref[...] = jnp.where(first, rows[0], rows[1])
    right_too_ref[...] = jnp.where(first, rows[1], rows[0])


def products(lefts, rights):
    right_high, right_low = split(jnp.concatenate([right[...] for right in rights], 0))
    for block, left in enumerate(lefts):
        left_high, left_low = split(left[...])
        product = dot(left_high, right_high) + dot(left_high, right_low) + dot(left_low, right_high)
        yield block, product * F32(2.0**-14)


def half_gram_kernel(own_ref, far_ref, up_ref, down_ref, right_ref, right_too_ref, out_ref):
    for block, product in products((own_ref, far_ref, up_ref, down_ref), (right_ref, right_too_ref)):
        out_ref[block * 128 : block * 128 + 128, :] = product


def gram_kernel(column_ref, half_ref, own_ref, far_ref, up_ref, down_ref, right_ref, right_too_ref, out_ref):
    chip = jnp.right_shift(column_ref[0], 1)
    core = jnp.bitwise_and(column_ref[0], 1)
    for block, product in products((own_ref, far_ref, up_ref, down_ref), (right_ref, right_too_ref)):
        place = jnp.bitwise_and(chip + (0, 2, 3, 1)[block], 3) * 256
        for q in range(4):
            start = place + (q % 2) * 128 + (q // 2) * 32
            mine = pl.multiple_of(start + core * 64, 32)
            out_ref[pl.ds(mine, 32), :] = half_ref[block * 128 + q * 32 : block * 128 + q * 32 + 32, :]
            others = pl.multiple_of(start + (1 - core) * 64, 32)
            out_ref[pl.ds(others, 32), :] = product[q * 32 : q * 32 + 32]


def call(kernel, out_shape, scratch=(), **more):
    vmem = pl.BlockSpec(memory_space=pltpu.VMEM)
    many = isinstance(out_shape, (list, tuple))
    return pl.pallas_call(
        kernel,
        out_shape=out_shape,
        out_specs=[vmem] * len(out_shape) if many else vmem,
        scratch_shapes=list(scratch),
        compiler_params=pltpu.CompilerParams(vmem_limit_bytes=VMEM_LIMIT),
        **more,
    )


def shape(*dims):
    return jax.ShapeDtypeStruct(dims, F32)


def from_partner(x, axis, distance):
    return lax.ppermute(x, axis, [(i, i ^ distance) for i in range(lax.axis_size(axis))])


def around_ring(x, steps):
    pairs = []
    for device in range(512):
        rest, ring, core = device // 16, device // 2 % 8, device % 2
        pairs.append((device, rest * 16 + (ring + steps[core]) % 8 * 2 + core))
    return lax.ppermute(x, ("row", "col"), pairs)


def shards(matrix, signs, picks):
    chunks = call(chunk_kernel, shape(GROUPS * TILES, 2, 128))(
        matrix, signs[None, :], picks.reshape(2, 128)
    )
    chunks = lax.all_to_all(chunks.reshape(GROUPS, TILES, 2, 128), "row", 0, 0, tiled=True)
    block_table = np.kron(np.eye(4), sylvester(2 * GROUPS)).reshape(8, GROUPS, 8 * GROUPS)
    block_table = jnp.asarray(block_table.transpose(1, 0, 2).reshape(8 * GROUPS, 8 * GROUPS), BF16)
    lane_table = jnp.asarray(sylvester(LANES), BF16)
    picked = call(mix_kernel, shape(16 * GROUPS, 128), [pltpu.VMEM((8 * GROUPS, LANES), F32)])(
        chunks.reshape(GROUPS * TILES, 2, 128), block_table, lane_table
    )
    picked = picked.reshape(GROUPS, 16, 128)
    picked = lax.all_to_all(picked, "row", 0, 0, tiled=True).reshape(16 * GROUPS, 128)

    vmem = pl.BlockSpec(memory_space=pltpu.VMEM)
    smem = pl.BlockSpec(memory_space=pltpu.SMEM)
    y_high = jnp.bitwise_and(lax.axis_index("row"), 1).astype(jnp.int32)[None]
    me = lax.axis_index("col").astype(jnp.int32)[None]
    places = [smem, smem, vmem]
    after = pl.BlockSpec(memory_space=pl.ANY)
    far_left = call(far_kernel, shape(128, 512), in_specs=places)(y_high, me, picked)
    far = around_ring(far_left, (2, 6))
    own, up, down = call(near_kernel, [shape(128, 512)] * 3, in_specs=[*places, after])(
        y_high, me, picked, far_left
    )
    sketch, *right = call(
        order_kernel, [shape(256, 256)] * 3, in_specs=[smem, vmem, after]
    )(y_high, picked, own)
    up, down = around_ring(up, (1, 1)), around_ring(down, (7, 7))
    other = [from_partner(part, "col", 1) for part in right]
    half = call(
        half_gram_kernel,
        shape(512, 256),
        cost_estimate=pl.CostEstimate(flops=6 * 512 * 512 * 256, bytes_accessed=2 << 20, transcendentals=0),
    )(own, far, up, down, *right)
    gram = call(gram_kernel, shape(1024, 256), in_specs=[smem] + [vmem] * 7)(
        me, half, own, far, up, down, *other
    )

    near = [
        [(x * 16 + h * 4 + l * 2 + y) * 8 + c * 2 + core for x in range(4) for l in range(2) for core in range(2)]
        for h in range(4)
        for y in range(2)
        for c in range(4)
    ]
    far = [[x * 16 + h * 4 + l * 2 + y for h in range(4)] for x in range(4) for l in range(2) for y in range(2)]
    gram = lax.all_to_all(gram, ("row", "col"), 0, 0, axis_index_groups=near, tiled=True)
    gram = jnp.sum(gram.reshape(8, 2, 64, 256), 0).reshape(128, 256)
    gram = lax.all_to_all(gram, "row", 0, 0, axis_index_groups=far, tiled=True)
    gram = jnp.sum(gram.reshape(4, 32, 256), 0)
    return sketch, gram


def solution(mesh):
    placed = (P("row", "col"), P("row"), P("row"))
    return jax.shard_map(
        shards,
        mesh=mesh,
        in_specs=placed,
        out_specs=(P("row", "col"), P("row", "col")),
        check_vma=False,
    )
```
